512 devices in a mesh: crop: 4 (over y_hi), res: 128 (over y_lo, z, x, core).
Axes of the slice: x: 4, y: 8 (y_hi: 4, y_lo: 2; y = y_hi * 2 + y_lo), z: 8, core: 2. Of those that a mesh axis runs over, the one named last changes fastest.
Arguments:
- alignment_features: bfloat16 [512, 512, 256], P(('crop', 'res')), parts along dimension 0, may hold values from -6 to 6
- standardizer_scaling: float32 [256], replicated, may hold values from 0.1 to 1.9
- first_factor_matrix: bfloat16 [256, 32], replicated, may hold values from -0.375 to 0.375
- second_factor_matrix: bfloat16 [256, 32], replicated, may hold values from -0.375 to 0.375
- final_mixing_matrix: bfloat16 [1024, 128], replicated, may hold values from -2 to 2
- final_offset: float32 [128], replicated, may hold values from -4 to 4
Outputs:
- pair_update: bfloat16 [2048, 512, 128], P(('crop', 'res')), parts along dimension 0
The draws below stay inside these ranges and needn't reach their ends.
There are 4 independent parts, one for each index of `crop`. The reference program is written for one: setup_inputs(seed, part) draws one part's arguments, and reference() takes and returns one part's arrays. A program takes and returns all parts, laid end to end along the dimension named above; an argument that names none is the same for every part. Nothing has to cross between parts.
All inputs are finite; a program needn't handle non-finite values.
Results may differ from the reference program's by a relative error of at most 0.0064.
Values may be sent and summed in bfloat16 or wider, within the bound.
No kernel may reach another device: no remote copies, remote signals or barrier semaphores. Data moves between devices by JAX's collectives and lax.ppermute only.
A program may use at most 64 MiB of HBM per device.

```python
import jax
import jax.numpy as jnp
from jax import lax

ALIGNMENT_DEPTH = 256
FACTOR_DEPTH = 32
PAIR_DEPTH = 128
ALIGNMENT_COUNT = 128
LOCAL_POSITIONS = 4
WINDOW_POSITIONS = 512


def block_scale(own_key, dims, cuts, low, largest):
    def one(axis_at, parts):
        heights = jax.random.uniform(jax.random.fold_in(jax.random.fold_in(own_key, 6), axis_at), (parts,), jnp.float32, low / len(cuts), largest / len(cuts))
        return jnp.repeat(jnp.exp(heights), dims[axis_at] // parts).reshape((-1,) + (1,) * (len(dims) - axis_at - 1))

    factor_of = one(*cuts[0])
    for cut in cuts[1:]:
        factor_of = factor_of * one(*cut)
    return factor_of


def bell_draw(key, dims, spread, most, split=(), held_as=jnp.bfloat16):
    array = spread * jax.random.normal(key, dims, jnp.float32)
    if split:
        array = array * block_scale(key, dims, split, -0.22, 0.18)
    return jnp.clip(array, -most, most).astype(held_as)


def setup_inputs(seed: int = 0, part: int = 0) -> dict:
    seeds = jax.random.split(jax.random.key(seed), 7)
    part_keys = jax.random.split(jax.random.fold_in(seeds[6], part), 7)
    alignment_features = bell_draw(part_keys[0], (ALIGNMENT_COUNT, WINDOW_POSITIONS, ALIGNMENT_DEPTH), 1.0, 6.0, ((0, 128),))
    standardizer_scaling = jnp.clip(1.0 + 0.18 * jax.random.normal(seeds[1], (ALIGNMENT_DEPTH,), jnp.float32), 0.1, 1.9)
    first_factor_matrix = bell_draw(seeds[2], (ALIGNMENT_DEPTH, FACTOR_DEPTH), ALIGNMENT_DEPTH ** -0.5, 0.375)
    second_factor_matrix = bell_draw(seeds[3], (ALIGNMENT_DEPTH, FACTOR_DEPTH), ALIGNMENT_DEPTH ** -0.5, 0.375)
    final_mixing_matrix = bell_draw(seeds[4], (FACTOR_DEPTH * FACTOR_DEPTH, PAIR_DEPTH), (FACTOR_DEPTH * FACTOR_DEPTH // ALIGNMENT_COUNT) ** -0.5, 2.0)
    final_offset = bell_draw(seeds[5], (PAIR_DEPTH,), 1.0, 4.0, (), jnp.float32)
    return {"alignment_features": alignment_features, "standardizer_scaling": standardizer_scaling, "first_factor_matrix": first_factor_matrix, "second_factor_matrix": second_factor_matrix, "final_mixing_matrix": final_mixing_matrix, "final_offset": final_offset}


def standardize_features(values, gain):
    mean = lax.optimization_barrier(jnp.mean(values, axis=-1, keepdims=True))
    centred = values - mean
    variance = lax.optimization_barrier(jnp.mean(centred * centred, axis=-1, keepdims=True))
    return centred * lax.rsqrt(variance + 1e-05) * gain

def reference(alignment_features, standardizer_scaling, first_factor_matrix, second_factor_matrix, final_mixing_matrix, final_offset):
    standardized_alignment = standardize_features(alignment_features.astype(jnp.float32), standardizer_scaling).astype(jnp.bfloat16)
    unrolled_tensor = standardized_alignment.reshape(ALIGNMENT_COUNT * WINDOW_POSITIONS, ALIGNMENT_DEPTH)
    first_factor = jnp.dot(unrolled_tensor, first_factor_matrix, preferred_element_type=jnp.float32).astype(jnp.bfloat16).reshape(ALIGNMENT_COUNT, WINDOW_POSITIONS, FACTOR_DEPTH)
    second_factor = jnp.dot(unrolled_tensor, second_factor_matrix, preferred_element_type=jnp.float32).astype(jnp.bfloat16).reshape(ALIGNMENT_COUNT, WINDOW_POSITIONS, FACTOR_DEPTH)
    second_factor_full = second_factor.astype(jnp.float32)
    tile_groups = first_factor.reshape(ALIGNMENT_COUNT, WINDOW_POSITIONS // LOCAL_POSITIONS, LOCAL_POSITIONS, FACTOR_DEPTH).transpose(1, 0, 2, 3)

    def one_block(first_factor_tile):
        tensor_products = jnp.einsum('pbm,pzk->bzmk', first_factor_tile.astype(jnp.float32), second_factor_full) / ALIGNMENT_COUNT
        tensor_products = tensor_products.astype(jnp.bfloat16).reshape(LOCAL_POSITIONS * WINDOW_POSITIONS, FACTOR_DEPTH * FACTOR_DEPTH)
        result = jnp.dot(tensor_products, final_mixing_matrix, preferred_element_type=jnp.float32) + final_offset
        return result.astype(jnp.bfloat16).reshape(LOCAL_POSITIONS, WINDOW_POSITIONS, PAIR_DEPTH)
    return lax.map(one_block, tile_groups).reshape(WINDOW_POSITIONS, WINDOW_POSITIONS, PAIR_DEPTH)
```

```python
import jax
import jax.numpy as jnp
from jax import lax
from jax.experimental import pallas as pl
from jax.experimental.pallas import tpu as pltpu
from jax.sharding import Mesh, PartitionSpec as P

Y, Z, X, C = 2, 8, 4, 2
F32, BF16 = jnp.float32, jnp.bfloat16
CHIP = ("y", "z", "x")
SLAB = ("y", "x", "c")
ALL = ("crop", "y", "z", "x", "c")


def project_kernel(x_ref, gain_ref, first_ref, second_ref, message_ref, rows_ref):
    x = x_ref[...].astype(F32)
    mean = jnp.mean(x, axis=-1, keepdims=True)
    centred = x - mean
    variance = jnp.mean(centred * centred, axis=-1, keepdims=True)
    normed = (centred * lax.rsqrt(variance + 1e-05) * gain_ref[...]).astype(BF16)
    first = first_ref[...]
    first4 = jnp.concatenate([first] * 4, axis=1)
    rows_ref[...] = jnp.dot(normed, first4, preferred_element_type=F32)
    group = lax.broadcasted_iota(jnp.int32, (128, 128), 1) // 32
    left = rows_ref[pl.ds(0, 128, stride=4), :]
    for r in range(1, 4):
        left = jnp.where(group == r, rows_ref[pl.ds(r, 128, stride=4), :], left)
    right = lax.dot_general(
        second_ref[...], normed, (((0,), (1,)), ((), ())), preferred_element_type=F32
    )
    low = lax.broadcasted_iota(jnp.int32, (16, 128), 1) < 64
    lefts = []
    for z in range(Z):
        lefts.append(
            jnp.concatenate([left[z * 8 : z * 8 + 8], left[64 + z * 8 : 72 + z * 8]], axis=0).astype(BF16)
        )
    for pair in range(4):
        head = right[:16, pair * 128 : pair * 128 + 128]
        tail = right[16:, pair * 128 : pair * 128 + 128]
        even = jnp.where(low, head, pltpu.roll(tail, 64, 1)).astype(BF16)
        odd = jnp.where(low, pltpu.roll(head, 64, 1), tail).astype(BF16)
        for which, block in ((2 * pair, even), (2 * pair + 1, odd)):
            y, xx = which // X, which % X
            for z in range(Z):
                at = (y * Z + z) * X + xx
                message_ref[at, :16, :] = lefts[z]
                message_ref[at, 16:, :] = block


def pair_kernel(core_ref, own_ref, other_ref, mix_ref, offset_ref, out_ref, flat_ref, wide_ref, lhs_ref, right_ref, outer_ref):
    core = core_ref[0]
    wide_ref[...] = mix_ref[...].astype(F32)
    mixer = jnp.concatenate(
        [wide_ref[pl.ds(e, 32, stride=32), :] for e in range(32)], axis=0
    ).T.astype(BF16)
    flat_ref[: 64 * 32] = own_ref[...].astype(F32).reshape(64 * 32, 128)
    flat_ref[64 * 32 :] = other_ref[...].astype(F32).reshape(64 * 32, 128)
    for row in range(16):
        block = flat_ref[pl.ds(row, 128, stride=32), :].T
        half = jnp.where(core == 0, block[:64], block[64:]).astype(BF16)
        lhs_ref[row * 32 : row * 32 + 32, :128] = half[:32]
        lhs_ref[row * 32 : row * 32 + 32, 128:] = half[32:]
    low = lax.broadcasted_iota(jnp.int32, (128, 128), 1) < 64
    zero = jnp.zeros((128, 128), F32)
    for row in range(16):
        block = flat_ref[pl.ds(16 + row, 128, stride=32), :]
        rolled = pltpu.roll(block, 64, 1)
        for e, lower, upper in ((row, block, rolled), (row + 16, rolled, block)):
            right_ref[:128, e * 128 : e * 128 + 128] = jnp.where(low, lower, zero).astype(BF16)
            right_ref[128:, e * 128 : e * 128 + 128] = jnp.where(low, zero, upper).astype(BF16)
    for pair in range(16):
        product = jnp.dot(
            lhs_ref[...], right_ref[:, pair * 256 : pair * 256 + 256], preferred_element_type=F32
        ).astype(BF16)
        for half in range(2):
            e = pair * 2 + half
            for row in range(16):
                outer_ref[e * 32 : e * 32 + 32, row * 128 : row * 128 + 128] = product[
                    row * 32 : row * 32 + 32, half * 128 : half * 128 + 128
                ]
    for pair in range(8):
        result = jnp.dot(
            mixer, outer_ref[:, pair * 256 : pair * 256 + 256], preferred_element_type=F32
        )
        for half in range(2):
            block = result[:, half * 128 : half * 128 + 128].T
            out_ref[pair * 2 + half] = (block * (1.0 / 128) + offset_ref[...]).astype(BF16)


def body(x, gain, first, second, mix, offset):
    x = x.reshape(512, 256)
    message = pl.pallas_call(
        project_kernel,
        out_shape=jax.ShapeDtypeStruct((64, 32, 128), BF16),
        scratch_shapes=[pltpu.VMEM((512, 128), F32)],
        compiler_params=pltpu.CompilerParams(vmem_limit_bytes=32 * 1024 * 1024),
    )(x, gain.reshape(1, 256), first, second)
    own = lax.all_to_all(message, CHIP, split_axis=0, concat_axis=0, tiled=True)
    other = lax.ppermute(own, "c", [(0, 1), (1, 0)])
    core = lax.axis_index("c").reshape(1)
    vmem = pl.BlockSpec(memory_space=pltpu.VMEM)
    tile = pl.pallas_call(
        pair_kernel,
        out_shape=jax.ShapeDtypeStruct((16, 128, 128), BF16),
        in_specs=[pl.BlockSpec(memory_space=pltpu.SMEM)] + [vmem] * 4,
        out_specs=vmem,
        scratch_shapes=[
            pltpu.VMEM((128 * 32, 128), F32),
            pltpu.VMEM((1024, 128), F32),
            pltpu.VMEM((512, 256), BF16),
            pltpu.VMEM((256, 4096), BF16),
            pltpu.VMEM((1024, 2048), BF16),
        ],
        compiler_params=pltpu.CompilerParams(vmem_limit_bytes=48 * 1024 * 1024),
    )(core, own, other, mix, offset.reshape(1, 128))
    got = lax.all_to_all(tile, SLAB, split_axis=0, concat_axis=0, tiled=True)
    got = got.reshape(Y, X, C, 2, 64, 128).transpose(2, 3, 0, 1, 4, 5)
    return got.reshape(4, 512, 128)


def solution(mesh):
    fine = Mesh(mesh.devices.reshape(mesh.devices.shape[0], Y, Z, X, C), ALL)
    split = P(ALL, None, None)
    return jax.shard_map(
        body, mesh=fine, in_specs=(split, P(), P(), P(), P(), P()), out_specs=split, check_vma=False
    )
```

```python
import jax
import jax.numpy as jnp
from jax import lax
from jax.experimental import pallas as pl
from jax.experimental.pallas import tpu as pltpu
from jax.sharding import Mesh, PartitionSpec as P

Y, Z, X, C = 2, 8, 4, 2
F32, BF16 = jnp.float32, jnp.bfloat16
CHIP = ("y", "z", "x")
COLUMN = ("y", "x")
ALL = ("crop", "y", "z", "x", "c")
NT = (((1,), (1,)), ((), ()))
MIB = 1024 * 1024


def project_kernel(x_hbm, gain_hbm, first_hbm, second_hbm, message_ref, x_ref, gain_ref, first_ref, second_ref, rows_ref, sems):
    small = [
        pltpu.make_async_copy(gain_hbm, gain_ref, sems.at[4]),
        pltpu.make_async_copy(first_hbm, first_ref, sems.at[5]),
        pltpu.make_async_copy(second_hbm, second_ref, sems.at[6]),
    ]
    chunks = [
        pltpu.make_async_copy(x_hbm.at[pl.ds(k * 128, 128)], x_ref.at[pl.ds(k * 128, 128)], sems.at[k])
        for k in range(4)
    ]
    for copy in [chunks[0]] + small + chunks[1:]:
        copy.start()
    low = lax.broadcasted_iota(jnp.int32, (16, 128), 1) < 64
    for k in range(4):
        chunks[k].wait()
        if k == 0:
            for copy in small:
                copy.wait()
            first4 = jnp.concatenate([first_ref[...]] * 4, axis=0)
        x = x_ref[k * 128 : k * 128 + 128].astype(F32)
        mean = jnp.mean(x, axis=-1, keepdims=True)
        centred = x - mean
        variance = jnp.mean(centred * centred, axis=-1, keepdims=True)
        normed = (centred * lax.rsqrt(variance + 1e-05) * gain_ref[...]).astype(BF16)
        rows_ref[k * 128 : k * 128 + 128] = lax.dot_general(normed, first4, NT, preferred_element_type=F32)
        right = lax.dot_general(second_ref[...], normed, NT, preferred_element_type=F32)
        head, tail = right[:16], right[16:]
        even = jnp.where(low, head, pltpu.roll(tail, 64, 1)).astype(BF16)
        odd = jnp.where(low, pltpu.roll(head, 64, 1), tail).astype(BF16)
        for which, block in ((2 * k, even), (2 * k + 1, odd)):
            for z in range(Z):
                message_ref[(which // X * Z + z) * X + which % X, 16:, :] = block
    group = lax.broadcasted_iota(jnp.int32, (128, 128), 1) // 32
    left = rows_ref[pl.ds(0, 128, stride=4), :]
    for r in range(1, 4):
        left = jnp.where(group == r, rows_ref[pl.ds(r, 128, stride=4), :], left)
    for z in range(Z):
        block = jnp.concatenate([left[z * 8 : z * 8 + 8], left[64 + z * 8 : 72 + z * 8]], axis=0).astype(BF16)
        for y in range(Y):
            for xx in range(X):
                message_ref[(y * Z + z) * X + xx, :16, :] = block


def spread(core, half_ref, flat_ref, lhs_ref, right_ref):
    flat_ref[...] = half_ref[...].astype(F32).reshape(64 * 32, 128)
    for owner in range(8):
        block = flat_ref[pl.ds(owner * 2 + core, 64, stride=32), :]
        both = jnp.concatenate([block, pltpu.roll(block, 96, 1)], axis=0).T.astype(BF16)
        lhs_ref[owner * 64 : owner * 64 + 32] = both[:32]
        lhs_ref[owner * 64 + 32 : owner * 64 + 64] = both[64:96]
    low = lax.broadcasted_iota(jnp.int32, (64, 128), 1) < 64
    zero = jnp.zeros((64, 128), F32)
    for row in range(16):
        block = flat_ref[pl.ds(16 + row, 64, stride=32), :]
        rolled = pltpu.roll(block, 64, 1)
        for e, lower, upper in ((row, block, rolled), (row + 16, rolled, block)):
            right_ref[:64, e * 128 : e * 128 + 128] = jnp.where(low, lower, zero).astype(BF16)
            right_ref[64:, e * 128 : e * 128 + 128] = jnp.where(low, zero, upper).astype(BF16)


def own_kernel(core_ref, own_ref, mix_ref, lhs_ref, right_ref, mixer_ref, flat_ref, wide_ref):
    wide_ref[...] = mix_ref[...].astype(F32)
    for e in range(0, 32, 4):
        rows = [wide_ref[pl.ds(e + k, 32, stride=32), :] for k in range(4)]
        mixer_ref[:, e * 32 : e * 32 + 128] = jnp.concatenate(rows, axis=0).T.astype(BF16)
    spread(core_ref[0], own_ref, flat_ref, lhs_ref, right_ref)


def pair_kernel(core_ref, other_ref, lhs_ref, right_ref, mixer_ref, offset_hbm, out_ref, flat_ref, lhs2_ref, right2_ref, outer_ref, offset_ref, sem):
    copy = pltpu.make_async_copy(offset_hbm, offset_ref, sem)
    copy.start()
    spread(core_ref[0], other_ref, flat_ref, lhs2_ref, right2_ref)
    lhs = jnp.concatenate([lhs_ref[...], lhs2_ref[...]], axis=1)
    for pair in range(16):
        at = slice(pair * 256, pair * 256 + 256)
        right = jnp.concatenate([right_ref[:, at], right2_ref[:, at]], axis=0)
        product = jnp.dot(lhs, right, preferred_element_type=F32).astype(BF16)
        for half in range(2):
            e = pair * 2 + half
            for row in range(16):
                outer_ref[e * 32 : e * 32 + 32, row * 128 : row * 128 + 128] = product[
                    row * 32 : row * 32 + 32, half * 128 : half * 128 + 128
                ]
    copy.wait()
    offset = offset_ref[...]
    for pair in range(8):
        result = jnp.dot(
            mixer_ref[...], outer_ref[:, pair * 256 : pair * 256 + 256], preferred_element_type=F32
        )
        for half in range(2):
            block = result[:, half * 128 : half * 128 + 128].T
            out_ref[pair * 2 + half] = (block * (1.0 / 128) + offset).astype(BF16)


def in_hbm(array):
    return pltpu.with_memory_space_constraint(array, pltpu.HBM)


def body(x, gain, first, second, mix, offset):
    hbm = pl.BlockSpec(memory_space=pltpu.HBM)
    vmem = pl.BlockSpec(memory_space=pltpu.VMEM)
    smem = pl.BlockSpec(memory_space=pltpu.SMEM)
    message = pl.pallas_call(
        project_kernel,
        out_shape=jax.ShapeDtypeStruct((64, 32, 128), BF16),
        in_specs=[hbm] * 4,
        out_specs=vmem,
        scratch_shapes=[
            pltpu.VMEM((512, 256), BF16),
            pltpu.VMEM((1, 256), F32),
            pltpu.VMEM((32, 256), BF16),
            pltpu.VMEM((32, 256), BF16),
            pltpu.VMEM((512, 128), F32),
            pltpu.SemaphoreType.DMA((7,)),
        ],
        compiler_params=pltpu.CompilerParams(vmem_limit_bytes=32 * MIB),
    )(in_hbm(x.reshape(512, 256)), in_hbm(gain.reshape(1, 256)), in_hbm(first.T), in_hbm(second.T))
    own = lax.all_to_all(message, CHIP, split_axis=0, concat_axis=0, tiled=True)
    other = lax.ppermute(own, "c", [(0, 1), (1, 0)])
    core = lax.axis_index("c").reshape(1)
    lhs, right, mixer = pl.pallas_call(
        own_kernel,
        out_shape=(
            jax.ShapeDtypeStruct((512, 128), BF16),
            jax.ShapeDtypeStruct((128, 4096), BF16),
            jax.ShapeDtypeStruct((128, 1024), BF16),
        ),
        in_specs=[smem, vmem, vmem],
        out_specs=(vmem, vmem, vmem),
        scratch_shapes=[pltpu.VMEM((64 * 32, 128), F32), pltpu.VMEM((1024, 128), F32)],
        compiler_params=pltpu.CompilerParams(vmem_limit_bytes=32 * MIB),
        cost_estimate=pl.CostEstimate(flops=2_000_000, bytes_accessed=2_000_000, transcendentals=0),
    )(core, own, mix)
    tile = pl.pallas_call(
        pair_kernel,
        out_shape=jax.ShapeDtypeStruct((16, 128, 128), BF16),
        in_specs=[smem, vmem, vmem, vmem, vmem, hbm],
        out_specs=vmem,
        scratch_shapes=[
            pltpu.VMEM((64 * 32, 128), F32),
            pltpu.VMEM((512, 128), BF16),
            pltpu.VMEM((128, 4096), BF16),
            pltpu.VMEM((1024, 2048), BF16),
            pltpu.VMEM((1, 128), F32),
            pltpu.SemaphoreType.DMA,
        ],
        compiler_params=pltpu.CompilerParams(vmem_limit_bytes=32 * MIB),
    )(core, other, lhs, right, mixer, in_hbm(offset.reshape(1, 128)))
    tile = tile.reshape(8, 4, 64, 128)
    got = lax.all_to_all(tile, COLUMN, split_axis=0, concat_axis=0, tiled=True)
    return got.transpose(1, 0, 2, 3).reshape(4, 512, 128)


def solution(mesh):
    fine = Mesh(mesh.devices.reshape(mesh.devices.shape[0], Y, Z, X, C), ALL)
    split = P(ALL, None, None)
    return jax.shard_map(
        body, mesh=fine, in_specs=(split, P(), P(), P(), P(), P()), out_specs=split, check_vma=False
    )
```

```python
import jax
import jax.numpy as jnp
from jax import lax
from jax.experimental import pallas as pl
from jax.experimental.pallas import tpu as pltpu
from jax.sharding import Mesh, PartitionSpec as P

Y, Z, X, C = 2, 8, 4, 2
F32, BF16 = jnp.float32, jnp.bfloat16
CHIP = ("y", "z", "x")
COLUMN = ("y", "x")
ALL = ("crop", "y", "z", "x", "c")
NT = (((1,), (1,)), ((), ()))
MIB = 1024 * 1024


def project_kernel(x_hbm, gain_hbm, first_hbm, second_hbm, message_ref, x_ref, gain_ref, first_ref, second_ref, rows_ref, sems):
    small = [
        pltpu.make_async_copy(gain_hbm, gain_ref, sems.at[4]),
        pltpu.make_async_copy(first_hbm, first_ref, sems.at[5]),
        pltpu.make_async_copy(second_hbm, second_ref, sems.at[6]),
    ]
    chunks = [
        pltpu.make_async_copy(x_hbm.at[pl.ds(k * 128, 128)], x_ref.at[pl.ds(k * 128, 128)], sems.at[k])
        for k in range(4)
    ]
    for copy in chunks + small:
        copy.start()
    for copy in chunks + small:
        copy.wait()
    low = lax.broadcasted_iota(jnp.int32, (16, 128), 1) < 64
    first4 = jnp.concatenate([first_ref[...]] * 4, axis=0)
    for k in range(4):
        x = x_ref[k * 128 : k * 128 + 128].astype(F32)
        mean = jnp.mean(x, axis=-1, keepdims=True)
        centred = x - mean
        variance = jnp.mean(centred * centred, axis=-1, keepdims=True)
        normed = (centred * lax.rsqrt(variance + 1e-05) * gain_ref[...]).astype(BF16)
        rows_ref[k * 128 : k * 128 + 128] = lax.dot_general(normed, first4, NT, preferred_element_type=F32)
        right = lax.dot_general(second_ref[...], normed, NT, preferred_element_type=F32)
        head, tail = right[:16], right[16:]
        even = jnp.where(low, head, pltpu.roll(tail, 64, 1)).astype(BF16)
        odd = jnp.where(low, pltpu.roll(head, 64, 1), tail).astype(BF16)
        for which, block in ((2 * k, even), (2 * k + 1, odd)):
            for z in range(Z):
                message_ref[(which // X * Z + z) * X + which % X, 16:, :] = block
    group = lax.broadcasted_iota(jnp.int32, (128, 128), 1) // 32
    left = rows_ref[pl.ds(0, 128, stride=4), :]
    for r in range(1, 4):
        left = jnp.where(group == r, rows_ref[pl.ds(r, 128, stride=4), :], left)
    for z in range(Z):
        block = jnp.concatenate([left[z * 8 : z * 8 + 8], left[64 + z * 8 : 72 + z * 8]], axis=0).astype(BF16)
        for y in range(Y):
            for xx in range(X):
                message_ref[(y * Z + z) * X + xx, :16, :] = block


def spread(core, half_ref, flat_ref, lhs_ref, right_ref):
    flat_ref[...] = half_ref[...].astype(F32).reshape(64 * 32, 128)
    for owner in range(8):
        block = flat_ref[pl.ds(owner * 2 + core, 64, stride=32), :]
        both = jnp.concatenate([block, pltpu.roll(block, 96, 1)], axis=0).T.astype(BF16)
        lhs_ref[owner * 64 : owner * 64 + 32] = both[:32]
        lhs_ref[owner * 64 + 32 : owner * 64 + 64] = both[64:96]
    low = lax.broadcasted_iota(jnp.int32, (64, 128), 1) < 64
    zero = jnp.zeros((64, 128), F32)
    for row in range(16):
        block = flat_ref[pl.ds(16 + row, 64, stride=32), :]
        rolled = pltpu.roll(block, 64, 1)
        for e, lower, upper in ((row, block, rolled), (row + 16, rolled, block)):
            right_ref[:64, e * 128 : e * 128 + 128] = jnp.where(low, lower, zero).astype(BF16)
            right_ref[64:, e * 128 : e * 128 + 128] = jnp.where(low, zero, upper).astype(BF16)


def own_kernel(core_ref, own_ref, mix_ref, lhs_ref, right_ref, mixer_ref, flat_ref, wide_ref):
    wide_ref[...] = mix_ref[...].astype(F32)
    for e in range(0, 32, 4):
        rows = [wide_ref[pl.ds(e + k, 32, stride=32), :] for k in range(4)]
        mixer_ref[:, e * 32 : e * 32 + 128] = jnp.concatenate(rows, axis=0).T.astype(BF16)
    spread(core_ref[0], own_ref, flat_ref, lhs_ref, right_ref)


def pair_kernel(core_ref, other_ref, lhs_ref, right_ref, mixer_ref, offset_hbm, out_ref, flat_ref, lhs2_ref, right2_ref, outer_ref, offset_ref, sem):
    copy = pltpu.make_async_copy(offset_hbm, offset_ref, sem)
    copy.start()
    spread(core_ref[0], other_ref, flat_ref, lhs2_ref, right2_ref)
    lhs = jnp.concatenate([lhs_ref[...], lhs2_ref[...]], axis=1)
    for pair in range(16):
        at = slice(pair * 256, pair * 256 + 256)
        right = jnp.concatenate([right_ref[:, at], right2_ref[:, at]], axis=0)
        product = jnp.dot(lhs, right, preferred_element_type=F32).astype(BF16)
        for half in range(2):
            e = pair * 2 + half
            for row in range(16):
                outer_ref[e * 32 : e * 32 + 32, row * 128 : row * 128 + 128] = product[
                    row * 32 : row * 32 + 32, half * 128 : half * 128 + 128
                ]
    copy.wait()
    offset = offset_ref[...]
    for pair in range(8):
        result = jnp.dot(
            mixer_ref[...], outer_ref[:, pair * 256 : pair * 256 + 256], preferred_element_type=F32
        )
        for half in range(2):
            block = result[:, half * 128 : half * 128 + 128].T
            out_ref[pair * 2 + half] = (block * (1.0 / 128) + offset).astype(BF16)


def in_hbm(array):
    return pltpu.with_memory_space_constraint(array, pltpu.HBM)


def body(x, gain, first, second, mix, offset):
    hbm = pl.BlockSpec(memory_space=pltpu.HBM)
    vmem = pl.BlockSpec(memory_space=pltpu.VMEM)
    smem = pl.BlockSpec(memory_space=pltpu.SMEM)
    message = pl.pallas_call(
        project_kernel,
        out_shape=jax.ShapeDtypeStruct((64, 32, 128), BF16),
        in_specs=[hbm] * 4,
        out_specs=vmem,
        scratch_shapes=[
            pltpu.VMEM((512, 256), BF16),
            pltpu.VMEM((1, 256), F32),
            pltpu.VMEM((32, 256), BF16),
            pltpu.VMEM((32, 256), BF16),
            pltpu.VMEM((512, 128), F32),
            pltpu.SemaphoreType.DMA((7,)),
        ],
        compiler_params=pltpu.CompilerParams(vmem_limit_bytes=32 * MIB),
    )(in_hbm(x.reshape(512, 256)), in_hbm(gain.reshape(1, 256)), in_hbm(first.T), in_hbm(second.T))
    own = lax.all_to_all(message, CHIP, split_axis=0, concat_axis=0, tiled=True)
    other = lax.ppermute(own, "c", [(0, 1), (1, 0)])
    core = lax.axis_index("c").reshape(1)
    lhs, right, mixer = pl.pallas_call(
        own_kernel,
        out_shape=(
            jax.ShapeDtypeStruct((512, 128), BF16),
            jax.ShapeDtypeStruct((128, 4096), BF16),
            jax.ShapeDtypeStruct((128, 1024), BF16),
        ),
        in_specs=[smem, vmem, vmem],
        out_specs=(vmem, vmem, vmem),
        scratch_shapes=[pltpu.VMEM((64 * 32, 128), F32), pltpu.VMEM((1024, 128), F32)],
        compiler_params=pltpu.CompilerParams(vmem_limit_bytes=32 * MIB),
        cost_estimate=pl.CostEstimate(flops=2_000_000, bytes_accessed=2_000_000, transcendentals=0),
    )(core, own, mix)
    tile = pl.pallas_call(
        pair_kernel,
        out_shape=jax.ShapeDtypeStruct((16, 128, 128), BF16),
        in_specs=[smem, vmem, vmem, vmem, vmem, hbm],
        out_specs=vmem,
        scratch_shapes=[
            pltpu.VMEM((64 * 32, 128), F32),
            pltpu.VMEM((512, 128), BF16),
            pltpu.VMEM((128, 4096), BF16),
            pltpu.VMEM((1024, 2048), BF16),
            pltpu.VMEM((1, 128), F32),
            pltpu.SemaphoreType.DMA,
        ],
        compiler_params=pltpu.CompilerParams(vmem_limit_bytes=32 * MIB),
    )(core, other, lhs, right, mixer, in_hbm(offset.reshape(1, 128)))
    tile = tile.reshape(8, 4, 64, 128)
    got = lax.all_to_all(tile, COLUMN, split_axis=0, concat_axis=0, tiled=True)
    return got.transpose(1, 0, 2, 3).reshape(4, 512, 128)


def solution(mesh):
    fine = Mesh(mesh.devices.reshape(mesh.devices.shape[0], Y, Z, X, C), ALL)
    split = P(ALL, None, None)
    return jax.shard_map(
        body, mesh=fine, in_specs=(split, P(), P(), P(), P(), P()), out_specs=split, check_vma=False
    )
```

```python
import jax
import jax.numpy as jnp
from jax import lax
from jax.experimental import pallas as pl
from jax.experimental.pallas import tpu as pltpu
from jax.sharding import Mesh, PartitionSpec as P

Y, Z, X, C = 2, 8, 4, 2
F32, BF16 = jnp.float32, jnp.bfloat16
CHIP = ("y", "z", "x")
COLUMN = ("y", "x")
ALL = ("crop", "y", "z", "x", "c")
NT = (((1,), (1,)), ((), ()))
MIB = 1024 * 1024


def project_kernel(x_hbm, gain_hbm, first_hbm, second_hbm, offset_hbm, message_ref, offset_ref, x_ref, gain_ref, first_ref, second_ref, rows_ref, sems):
    small = [
        pltpu.make_async_copy(gain_hbm, gain_ref, sems.at[4]),
        pltpu.make_async_copy(first_hbm, first_ref, sems.at[5]),
        pltpu.make_async_copy(second_hbm, second_ref, sems.at[6]),
        pltpu.make_async_copy(offset_hbm, offset_ref, sems.at[7]),
    ]
    chunks = [
        pltpu.make_async_copy(x_hbm.at[pl.ds(k * 128, 128)], x_ref.at[pl.ds(k * 128, 128)], sems.at[k])
        for k in range(4)
    ]
    for copy in chunks + small:
        copy.start()
    for copy in chunks + small:
        copy.wait()
    low = lax.broadcasted_iota(jnp.int32, (16, 128), 1) < 64
    first4 = jnp.concatenate([first_ref[...]] * 4, axis=0)
    for k in range(4):
        x = x_ref[k * 128 : k * 128 + 128].astype(F32)
        mean = jnp.mean(x, axis=-1, keepdims=True)
        centred = x - mean
        variance = jnp.mean(centred * centred, axis=-1, keepdims=True)
        normed = (centred * lax.rsqrt(variance + 1e-05) * gain_ref[...]).astype(BF16)
        rows_ref[k * 128 : k * 128 + 128] = lax.dot_general(normed, first4, NT, preferred_element_type=F32)
        right = lax.dot_general(second_ref[...], normed, NT, preferred_element_type=F32)
        head, tail = right[:16], right[16:]
        even = jnp.where(low, head, pltpu.roll(tail, 64, 1)).astype(BF16)
        odd = jnp.where(low, pltpu.roll(head, 64, 1), tail).astype(BF16)
        for which, block in ((2 * k, even), (2 * k + 1, odd)):
            for z in range(Z):
                message_ref[(which // X * Z + z) * X + which % X, 16:, :] = block
    group = lax.broadcasted_iota(jnp.int32, (128, 128), 1) // 32
    left = rows_ref[pl.ds(0, 128, stride=4), :]
    for r in range(1, 4):
        left = jnp.where(group == r, rows_ref[pl.ds(r, 128, stride=4), :], left)
    for z in range(Z):
        block = jnp.concatenate([left[z * 8 : z * 8 + 8], left[64 + z * 8 : 72 + z * 8]], axis=0).astype(BF16)
        for y in range(Y):
            for xx in range(X):
                message_ref[(y * Z + z) * X + xx, :16, :] = block


def spread_left(core, flat_ref, write):
    for owner in range(8):
        block = flat_ref[pl.ds(owner * 2 + core, 64, stride=32), :]
        both = jnp.concatenate([block, pltpu.roll(block, 96, 1)], axis=0).T.astype(BF16)
        write(owner * 64, both[:32])
        write(owner * 64 + 32, both[64:96])


def spread_right(row, flat_ref):
    low = lax.broadcasted_iota(jnp.int32, (64, 128), 1) < 64
    zero = jnp.zeros((64, 128), F32)
    block = flat_ref[pl.ds(16 + row, 64, stride=32), :]
    rolled = pltpu.roll(block, 64, 1)
    upper = jnp.concatenate([jnp.where(low, block, zero), jnp.where(low, rolled, zero)], axis=1)
    lower = jnp.concatenate([jnp.where(low, zero, rolled), jnp.where(low, zero, block)], axis=1)
    return jnp.concatenate([upper, lower], axis=0).astype(BF16)


def own_kernel(core_ref, own_ref, mix_ref, lhs_ref, right_ref, mixer_ref, flat_ref, wide_ref):
    wide_ref[...] = mix_ref[...].astype(F32)
    for e in range(0, 32, 4):
        rows = [wide_ref[pl.ds(e + k, 32, stride=32), :] for k in range(4)]
        mixer_ref[:, e * 32 : e * 32 + 128] = jnp.concatenate(rows, axis=0).T.astype(BF16)
    flat_ref[...] = own_ref[...].astype(F32).reshape(64 * 32, 128)

    def write(at, value):
        lhs_ref[at : at + 32] = value

    spread_left(core_ref[0], flat_ref, write)
    for row in range(16):
        right_ref[:, row * 256 : row * 256 + 256] = spread_right(row, flat_ref)


def pair_kernel(core_ref, other_ref, lhs_ref, right_ref, mixer_ref, offset_ref, out_ref, flat_ref, both_ref, outer_ref):
    flat_ref[...] = other_ref[...].astype(F32).reshape(64 * 32, 128)

    def write(at, value):
        both_ref[at : at + 32, 128:] = value

    spread_left(core_ref[0], flat_ref, write)
    both_ref[:, :128] = lhs_ref[...]
    for row in range(16):
        right = jnp.concatenate(
            [right_ref[:, row * 256 : row * 256 + 256], spread_right(row, flat_ref)], axis=0
        )
        product = jnp.dot(both_ref[...], right, preferred_element_type=F32).astype(BF16)
        for half in range(2):
            e = row + 16 * half
            for owner in range(16):
                outer_ref[e * 32 : e * 32 + 32, owner * 128 : owner * 128 + 128] = product[
                    owner * 32 : owner * 32 + 32, half * 128 : half * 128 + 128
                ]
    for pair in range(8):
        result = jnp.dot(
            mixer_ref[...], outer_ref[:, pair * 256 : pair * 256 + 256], preferred_element_type=F32
        )
        for half in range(2):
            block = result[:, half * 128 : half * 128 + 128].T
            out_ref[pair * 2 + half] = (block * (1.0 / 128) + offset_ref[...]).astype(BF16)


def in_hbm(array):
    return pltpu.with_memory_space_constraint(array, pltpu.HBM)


def body(x, gain, first, second, mix, offset):
    hbm = pl.BlockSpec(memory_space=pltpu.HBM)
    vmem = pl.BlockSpec(memory_space=pltpu.VMEM)
    smem = pl.BlockSpec(memory_space=pltpu.SMEM)
    message, bias = pl.pallas_call(
        project_kernel,
        out_shape=(
            jax.ShapeDtypeStruct((64, 32, 128), BF16),
            jax.ShapeDtypeStruct((1, 128), F32),
        ),
        in_specs=[hbm] * 5,
        out_specs=(vmem, vmem),
        scratch_shapes=[
            pltpu.VMEM((512, 256), BF16),
            pltpu.VMEM((1, 256), F32),
            pltpu.VMEM((32, 256), BF16),
            pltpu.VMEM((32, 256), BF16),
            pltpu.VMEM((512, 128), F32),
            pltpu.SemaphoreType.DMA((8,)),
        ],
        compiler_params=pltpu.CompilerParams(vmem_limit_bytes=32 * MIB),
    )(
        in_hbm(x.reshape(512, 256)),
        in_hbm(gain.reshape(1, 256)),
        in_hbm(first.T),
        in_hbm(second.T),
        in_hbm(offset.reshape(1, 128)),
    )
    own = lax.all_to_all(message, CHIP, split_axis=0, concat_axis=0, tiled=True)
    other = lax.ppermute(own, "c", [(0, 1), (1, 0)])
    core = lax.axis_index("c").reshape(1)
    lhs, right, mixer = pl.pallas_call(
        own_kernel,
        out_shape=(
            jax.ShapeDtypeStruct((512, 128), BF16),
            jax.ShapeDtypeStruct((128, 4096), BF16),
            jax.ShapeDtypeStruct((128, 1024), BF16),
        ),
        in_specs=[smem, vmem, vmem],
        out_specs=(vmem, vmem, vmem),
        scratch_shapes=[pltpu.VMEM((64 * 32, 128), F32), pltpu.VMEM((1024, 128), F32)],
        compiler_params=pltpu.CompilerParams(vmem_limit_bytes=32 * MIB),
        cost_estimate=pl.CostEstimate(flops=2_000_000, bytes_accessed=2_000_000, transcendentals=0),
    )(core, own, mix)
    tile = pl.pallas_call(
        pair_kernel,
        out_shape=jax.ShapeDtypeStruct((16, 128, 128), BF16),
        in_specs=[smem] + [vmem] * 5,
        out_specs=vmem,
        scratch_shapes=[
            pltpu.VMEM((64 * 32, 128), F32),
            pltpu.VMEM((512, 256), BF16),
            pltpu.VMEM((1024, 2048), BF16),
        ],
        compiler_params=pltpu.CompilerParams(vmem_limit_bytes=32 * MIB),
    )(core, other, lhs, right, mixer, bias)
    tile = tile.reshape(8, 4, 64, 128)
    got = lax.all_to_all(tile, COLUMN, split_axis=0, concat_axis=0, tiled=True)
    return got.transpose(1, 0, 2, 3).reshape(4, 512, 128)


def solution(mesh):
    fine = Mesh(mesh.devices.reshape(mesh.devices.shape[0], Y, Z, X, C), ALL)
    split = P(ALL, None, None)
    return jax.shard_map(
        body, mesh=fine, in_specs=(split, P(), P(), P(), P(), P()), out_specs=split, check_vma=False
    )
```

```python
import jax
import jax.numpy as jnp
from jax import lax
from jax.experimental import pallas as pl
from jax.experimental.pallas import tpu as pltpu
from jax.sharding import Mesh, PartitionSpec as P

Y, Z, X, C = 2, 8, 4, 2
F32, BF16 = jnp.float32, jnp.bfloat16
CHIP = ("y", "z", "x")
COLUMN = ("y", "x")
ALL = ("crop", "y", "z", "x", "c")
NT = (((1,), (1,)), ((), ()))
MIB = 1024 * 1024


def project_kernel(x_hbm, gain_hbm, first_hbm, second_hbm, offset_hbm, message_ref, offset_ref, x_ref, gain_ref, first_ref, second_ref, rows_ref, sems):
    small = [
        pltpu.make_async_copy(gain_hbm, gain_ref, sems.at[4]),
        pltpu.make_async_copy(first_hbm, first_ref, sems.at[5]),
        pltpu.make_async_copy(second_hbm, second_ref, sems.at[6]),
        pltpu.make_async_copy(offset_hbm, offset_ref, sems.at[7]),
    ]
    chunks = [
        pltpu.make_async_copy(x_hbm.at[pl.ds(k * 128, 128)], x_ref.at[pl.ds(k * 128, 128)], sems.at[k])
        for k in range(4)
    ]
    for copy in chunks + small:
        copy.start()
    for copy in chunks + small:
        copy.wait()
    low = lax.broadcasted_iota(jnp.int32, (16, 128), 1) < 64
    first4 = jnp.concatenate([first_ref[...]] * 4, axis=0)
    for k in range(4):
        x = x_ref[k * 128 : k * 128 + 128].astype(F32)
        mean = jnp.mean(x, axis=-1, keepdims=True)
        centred = x - mean
        variance = jnp.mean(centred * centred, axis=-1, keepdims=True)
        normed = (centred * lax.rsqrt(variance + 1e-05) * gain_ref[...]).astype(BF16)
        rows_ref[k * 128 : k * 128 + 128] = lax.dot_general(normed, first4, NT, preferred_element_type=F32)
        right = lax.dot_general(second_ref[...], normed, NT, preferred_element_type=F32)
        head, tail = right[:16], right[16:]
        even = jnp.where(low, head, pltpu.roll(tail, 64, 1)).astype(BF16)
        odd = jnp.where(low, pltpu.roll(head, 64, 1), tail).astype(BF16)
        for which, block in ((2 * k, even), (2 * k + 1, odd)):
            for z in range(Z):
                message_ref[(which // X * Z + z) * X + which % X, 16:, :] = block
    group = lax.broadcasted_iota(jnp.int32, (128, 128), 1) // 32
    left = rows_ref[pl.ds(0, 128, stride=4), :]
    for r in range(1, 4):
        left = jnp.where(group == r, rows_ref[pl.ds(r, 128, stride=4), :], left)
    for z in range(Z):
        block = jnp.concatenate([left[z * 8 : z * 8 + 8], left[64 + z * 8 : 72 + z * 8]], axis=0).astype(BF16)
        for y in range(Y):
            for xx in range(X):
                message_ref[(y * Z + z) * X + xx, :16, :] = block


def spread_left(core, flat_ref, write):
    for owner in range(8):
        block = flat_ref[pl.ds(owner * 2 + core, 64, stride=32), :]
        both = jnp.concatenate([block, pltpu.roll(block, 96, 1)], axis=0).T.astype(BF16)
        write(owner * 64, both[:32])
        write(owner * 64 + 32, both[64:96])


def spread_right(block):
    low = lax.broadcasted_iota(jnp.int32, (64, 128), 1) < 64
    zero = jnp.zeros((64, 128), F32)
    block = block.astype(F32)
    rolled = pltpu.roll(block, 64, 1)
    upper = jnp.concatenate([jnp.where(low, block, zero), jnp.where(low, rolled, zero)], axis=1)
    lower = jnp.concatenate([jnp.where(low, zero, rolled), jnp.where(low, zero, block)], axis=1)
    return jnp.concatenate([upper, lower], axis=0).astype(BF16)


def share_kernel(core_ref, own_ref, mix_ref, lhs_ref, share_ref, mixer_ref, flat_ref, wide_ref):
    flat_ref[...] = own_ref[...].astype(F32).reshape(64 * 32, 128)

    def write_own(at, value):
        lhs_ref[at : at + 32] = value

    def write_other(at, value):
        share_ref[at : at + 32] = value

    spread_left(core_ref[0], flat_ref, write_own)
    spread_left(1 - core_ref[0], flat_ref, write_other)
    for row in range(16):
        share_ref[512 + row * 64 : 576 + row * 64] = flat_ref[pl.ds(16 + row, 64, stride=32), :].astype(BF16)
    wide_ref[...] = mix_ref[...].astype(F32)
    for e in range(0, 32, 4):
        rows = [wide_ref[pl.ds(e + k, 32, stride=32), :] for k in range(4)]
        mixer_ref[:, e * 32 : e * 32 + 128] = jnp.concatenate(rows, axis=0).T.astype(BF16)


def pair_kernel(core_ref, shares_ref, lhs_ref, share_ref, mixer_ref, offset_ref, out_ref, both_ref, outer_ref):
    other = 1 - core_ref[0]
    both_ref[:, :128] = lhs_ref[...]
    both_ref[:, 128:] = shares_ref[other, :512]
    for row in range(16):
        at = slice(512 + row * 64, 576 + row * 64)
        right = jnp.concatenate([spread_right(share_ref[at]), spread_right(shares_ref[other, at])], axis=0)
        product = jnp.dot(both_ref[...], right, preferred_element_type=F32).astype(BF16)
        for half in range(2):
            e = row + 16 * half
            for owner in range(16):
                outer_ref[e * 32 : e * 32 + 32, owner * 128 : owner * 128 + 128] = product[
                    owner * 32 : owner * 32 + 32, half * 128 : half * 128 + 128
                ]
    for pair in range(8):
        result = jnp.dot(
            mixer_ref[...], outer_ref[:, pair * 256 : pair * 256 + 256], preferred_element_type=F32
        )
        for half in range(2):
            block = result[:, half * 128 : half * 128 + 128].T
            out_ref[pair * 2 + half] = (block * (1.0 / 128) + offset_ref[...]).astype(BF16)


def in_hbm(array):
    return pltpu.with_memory_space_constraint(array, pltpu.HBM)


def body(x, gain, first, second, mix, offset):
    hbm = pl.BlockSpec(memory_space=pltpu.HBM)
    vmem = pl.BlockSpec(memory_space=pltpu.VMEM)
    smem = pl.BlockSpec(memory_space=pltpu.SMEM)
    message, bias = pl.pallas_call(
        project_kernel,
        out_shape=(
            jax.ShapeDtypeStruct((64, 32, 128), BF16),
            jax.ShapeDtypeStruct((1, 128), F32),
        ),
        in_specs=[hbm] * 5,
        out_specs=(vmem, vmem),
        scratch_shapes=[
            pltpu.VMEM((512, 256), BF16),
            pltpu.VMEM((1, 256), F32),
            pltpu.VMEM((32, 256), BF16),
            pltpu.VMEM((32, 256), BF16),
            pltpu.VMEM((512, 128), F32),
            pltpu.SemaphoreType.DMA((8,)),
        ],
        compiler_params=pltpu.CompilerParams(vmem_limit_bytes=32 * MIB),
    )(
        in_hbm(x.reshape(512, 256)),
        in_hbm(gain.reshape(1, 256)),
        in_hbm(first.T),
        in_hbm(second.T),
        in_hbm(offset.reshape(1, 128)),
    )
    message, core = lax.optimization_barrier((message, lax.axis_index("c").reshape(1)))
    own = lax.all_to_all(message, CHIP, split_axis=0, concat_axis=0, tiled=True)
    lhs, share, mixer = pl.pallas_call(
        share_kernel,
        out_shape=(
            jax.ShapeDtypeStruct((512, 128), BF16),
            jax.ShapeDtypeStruct((1536, 128), BF16),
            jax.ShapeDtypeStruct((128, 1024), BF16),
        ),
        in_specs=[smem, vmem, vmem],
        out_specs=(vmem, vmem, vmem),
        scratch_shapes=[pltpu.VMEM((64 * 32, 128), F32), pltpu.VMEM((1024, 128), F32)],
        compiler_params=pltpu.CompilerParams(vmem_limit_bytes=32 * MIB),
    )(core, own, mix)
    shares = lax.all_gather(share, "c", axis=0, tiled=False)
    tile = pl.pallas_call(
        pair_kernel,
        out_shape=jax.ShapeDtypeStruct((16, 128, 128), BF16),
        in_specs=[smem] + [vmem] * 5,
        out_specs=vmem,
        scratch_shapes=[
            pltpu.VMEM((512, 256), BF16),
            pltpu.VMEM((1024, 2048), BF16),
        ],
        compiler_params=pltpu.CompilerParams(vmem_limit_bytes=32 * MIB),
    )(core, shares, lhs, share, mixer, bias)
    tile = tile.reshape(8, 4, 64, 128)
    got = lax.all_to_all(tile, COLUMN, split_axis=0, concat_axis=0, tiled=True)
    return got.transpose(1, 0, 2, 3).reshape(4, 512, 128)


def solution(mesh):
    fine = Mesh(mesh.devices.reshape(mesh.devices.shape[0], Y, Z, X, C), ALL)
    split = P(ALL, None, None)
    return jax.shard_map(
        body, mesh=fine, in_specs=(split, P(), P(), P(), P(), P()), out_specs=split, check_vma=False
    )
```

```python
import jax
import jax.numpy as jnp
from jax import lax
from jax.experimental import pallas as pl
from jax.experimental.pallas import tpu as pltpu
from jax.sharding import PartitionSpec as P

Y, Z, X, C = 2, 8, 4, 2
F32, BF16 = jnp.float32, jnp.bfloat16
ORDER = [(y, z, x) for y in range(Y) for z in reversed(range(Z)) for x in range(X)]
PLACE = [[[ORDER.index((y, z, x)) for x in range(X)] for z in range(Z)] for y in range(Y)]
CHIP = [[((y * Z + z) * X + x) * C + c for y, z, x in ORDER] for c in range(C)]
COLUMN = [[((y * Z + z) * X + x) * C + c for y in range(Y) for x in range(X)] for z in range(Z) for c in range(C)]
PAIR = [[2 * k, 2 * k + 1] for k in range(Y * Z * X)]
NT = (((1,), (1,)), ((), ()))
MIB = 1024 * 1024


def project_kernel(x_hbm, gain_hbm, first_hbm, second_hbm, offset_hbm, message_ref, offset_ref, x_ref, gain_ref, first_ref, second_ref, rows_ref, sems):
    small = [
        pltpu.make_async_copy(gain_hbm, gain_ref, sems.at[4]),
        pltpu.make_async_copy(first_hbm, first_ref, sems.at[5]),
        pltpu.make_async_copy(second_hbm, second_ref, sems.at[6]),
        pltpu.make_async_copy(offset_hbm, offset_ref, sems.at[7]),
    ]
    chunks = [
        pltpu.make_async_copy(x_hbm.at[pl.ds(k * 128, 128)], x_ref.at[pl.ds(k * 128, 128)], sems.at[k])
        for k in range(4)
    ]
    for copy in chunks + small:
        copy.start()
    for copy in chunks + small:
        copy.wait()
    low = lax.broadcasted_iota(jnp.int32, (16, 128), 1) < 64
    first4 = jnp.concatenate([first_ref[...]] * 4, axis=0)
    for k in range(4):
        x = x_ref[k * 128 : k * 128 + 128].astype(F32)
        mean = jnp.mean(x, axis=-1, keepdims=True)
        centred = x - mean
        variance = jnp.mean(centred * centred, axis=-1, keepdims=True)
        normed = (centred * lax.rsqrt(variance + 1e-05) * gain_ref[...]).astype(BF16)
        rows_ref[k * 128 : k * 128 + 128] = lax.dot_general(normed, first4, NT, preferred_element_type=F32)
        right = lax.dot_general(second_ref[...], normed, NT, preferred_element_type=F32)
        head, tail = right[:16], right[16:]
        even = jnp.where(low, head, pltpu.roll(tail, 64, 1)).astype(BF16)
        odd = jnp.where(low, pltpu.roll(head, 64, 1), tail).astype(BF16)
        for which, block in ((2 * k, even), (2 * k + 1, odd)):
            for z in range(Z):
                message_ref[PLACE[which // X][z][which % X], 16:, :] = block
    group = lax.broadcasted_iota(jnp.int32, (128, 128), 1) // 32
    left = rows_ref[pl.ds(0, 128, stride=4), :]
    for r in range(1, 4):
        left = jnp.where(group == r, rows_ref[pl.ds(r, 128, stride=4), :], left)
    for z in range(Z):
        block = jnp.concatenate([left[z * 8 : z * 8 + 8], left[64 + z * 8 : 72 + z * 8]], axis=0).astype(BF16)
        for y in range(Y):
            for xx in range(X):
                message_ref[PLACE[y][z][xx], :16, :] = block


def spread_left(core, flat_ref, write):
    for owner in range(8):
        block = flat_ref[pl.ds(owner * 2 + core, 64, stride=32), :]
        both = jnp.concatenate([block, pltpu.roll(block, 96, 1)], axis=0).T.astype(BF16)
        write(owner * 64, both[:32])
        write(owner * 64 + 32, both[64:96])


def spread_right(block):
    low = lax.broadcasted_iota(jnp.int32, (64, 128), 1) < 64
    zero = jnp.zeros((64, 128), F32)
    block = block.astype(F32)
    rolled = pltpu.roll(block, 64, 1)
    upper = jnp.concatenate([jnp.where(low, block, zero), jnp.where(low, rolled, zero)], axis=1)
    lower = jnp.concatenate([jnp.where(low, zero, rolled), jnp.where(low, zero, block)], axis=1)
    return jnp.concatenate([upper, lower], axis=0).astype(BF16)


def share_kernel(core_ref, own_ref, mix_ref, lhs_ref, share_ref, mixer_ref, flat_ref, wide_ref):
    flat_ref[...] = own_ref[...].astype(F32).reshape(64 * 32, 128)

    def write_own(at, value):
        lhs_ref[at : at + 32] = value

    def write_other(at, value):
        share_ref[at : at + 32] = value

    spread_left(core_ref[0], flat_ref, write_own)
    spread_left(1 - core_ref[0], flat_ref, write_other)
    for row in range(16):
        share_ref[512 + row * 64 : 576 + row * 64] = flat_ref[pl.ds(16 + row, 64, stride=32), :].astype(BF16)
    wide_ref[...] = mix_ref[...].astype(F32)
    for e in range(0, 32, 4):
        rows = [wide_ref[pl.ds(e + k, 32, stride=32), :] for k in range(4)]
        mixer_ref[:, e * 32 : e * 32 + 128] = jnp.concatenate(rows, axis=0).T.astype(BF16)


def pair_kernel(core_ref, shares_ref, lhs_ref, share_ref, mixer_ref, offset_ref, out_ref, both_ref, outer_ref):
    other = 1 - core_ref[0]
    both_ref[:, :128] = lhs_ref[...]
    both_ref[:, 128:] = shares_ref[other, :512]
    for row in range(16):
        at = slice(512 + row * 64, 576 + row * 64)
        right = jnp.concatenate([spread_right(share_ref[at]), spread_right(shares_ref[other, at])], axis=0)
        product = jnp.dot(both_ref[...], right, preferred_element_type=F32).astype(BF16)
        for half in range(2):
            e = row + 16 * half
            for owner in range(16):
                outer_ref[e * 32 : e * 32 + 32, owner * 128 : owner * 128 + 128] = product[
                    owner * 32 : owner * 32 + 32, half * 128 : half * 128 + 128
                ]
    for pair in range(8):
        result = jnp.dot(
            mixer_ref[...], outer_ref[:, pair * 256 : pair * 256 + 256], preferred_element_type=F32
        )
        for half in range(2):
            block = result[:, half * 128 : half * 128 + 128].T
            out_ref[pair * 2 + half] = (block * (1.0 / 128) + offset_ref[...]).astype(BF16)


def in_hbm(array):
    return pltpu.with_memory_space_constraint(array, pltpu.HBM)


def body(x, gain, first, second, mix, offset):
    hbm = pl.BlockSpec(memory_space=pltpu.HBM)
    vmem = pl.BlockSpec(memory_space=pltpu.VMEM)
    smem = pl.BlockSpec(memory_space=pltpu.SMEM)
    message, bias = pl.pallas_call(
        project_kernel,
        out_shape=(
            jax.ShapeDtypeStruct((64, 32, 128), BF16),
            jax.ShapeDtypeStruct((1, 128), F32),
        ),
        in_specs=[hbm] * 5,
        out_specs=(vmem, vmem),
        scratch_shapes=[
            pltpu.VMEM((512, 256), BF16),
            pltpu.VMEM((1, 256), F32),
            pltpu.VMEM((32, 256), BF16),
            pltpu.VMEM((32, 256), BF16),
            pltpu.VMEM((512, 128), F32),
            pltpu.SemaphoreType.DMA((8,)),
        ],
        compiler_params=pltpu.CompilerParams(vmem_limit_bytes=32 * MIB),
    )(
        in_hbm(x.reshape(512, 256)),
        in_hbm(gain.reshape(1, 256)),
        in_hbm(first.T),
        in_hbm(second.T),
        in_hbm(offset.reshape(1, 128)),
    )
    message, core = lax.optimization_barrier((message, (lax.axis_index("res") % C).reshape(1)))
    own = lax.all_to_all(message, "res", split_axis=0, concat_axis=0, tiled=True, axis_index_groups=CHIP)
    lhs, share, mixer = pl.pallas_call(
        share_kernel,
        out_shape=(
            jax.ShapeDtypeStruct((512, 128), BF16),
            jax.ShapeDtypeStruct((1536, 128), BF16),
            jax.ShapeDtypeStruct((128, 1024), BF16),
        ),
        in_specs=[smem, vmem, vmem],
        out_specs=(vmem, vmem, vmem),
        scratch_shapes=[pltpu.VMEM((64 * 32, 128), F32), pltpu.VMEM((1024, 128), F32)],
        compiler_params=pltpu.CompilerParams(vmem_limit_bytes=32 * MIB),
    )(core, own, mix)
    shares = lax.all_gather(share, "res", axis=0, tiled=False, axis_index_groups=PAIR)
    tile = pl.pallas_call(
        pair_kernel,
        out_shape=jax.ShapeDtypeStruct((16, 128, 128), BF16),
        in_specs=[smem] + [vmem] * 5,
        out_specs=vmem,
        scratch_shapes=[
            pltpu.VMEM((512, 256), BF16),
            pltpu.VMEM((1024, 2048), BF16),
        ],
        compiler_params=pltpu.CompilerParams(vmem_limit_bytes=32 * MIB),
    )(core, shares, lhs, share, mixer, bias)
    tile = tile.reshape(8, 4, 64, 128)
    got = lax.all_to_all(tile, "res", split_axis=0, concat_axis=0, tiled=True, axis_index_groups=COLUMN)
    return got.transpose(1, 0, 2, 3).reshape(4, 512, 128)


def solution(mesh):
    split = P(("crop", "res"), None, None)
    return jax.shard_map(
        body, mesh=mesh, in_specs=(split, P(), P(), P(), P(), P()), out_specs=split, check_vma=False
    )
```

```python
import jax
import jax.numpy as jnp
from jax import lax
from jax.experimental import pallas as pl
from jax.experimental.pallas import tpu as pltpu
from jax.sharding import PartitionSpec as P

Y, Z, X, C = 2, 8, 4, 2
F32, BF16 = jnp.float32, jnp.bfloat16
ORDER = [(y, z, x) for y in reversed(range(Y)) for z in reversed(range(Z)) for x in range(X)]
PLACE = [[[ORDER.index((y, z, x)) for x in range(X)] for z in range(Z)] for y in range(Y)]
CHIP = [[((y * Z + z) * X + x) * C + c for y, z, x in ORDER] for c in range(C)]
COLUMN = [[((y * Z + z) * X + x) * C + c for y in range(Y) for x in range(X)] for z in range(Z) for c in range(C)]
PAIR = [[2 * k, 2 * k + 1] for k in range(Y * Z * X)]
NT = (((1,), (1,)), ((), ()))
MIB = 1024 * 1024


def project_kernel(x_hbm, gain_hbm, first_hbm, second_hbm, offset_hbm, message_ref, offset_ref, x_ref, gain_ref, first_ref, second_ref, rows_ref, sems):
    small = [
        pltpu.make_async_copy(gain_hbm, gain_ref, sems.at[4]),
        pltpu.make_async_copy(first_hbm, first_ref, sems.at[5]),
        pltpu.make_async_copy(second_hbm, second_ref, sems.at[6]),
        pltpu.make_async_copy(offset_hbm, offset_ref, sems.at[7]),
    ]
    chunks = [
        pltpu.make_async_copy(x_hbm.at[pl.ds(k * 128, 128)], x_ref.at[pl.ds(k * 128, 128)], sems.at[k])
        for k in range(4)
    ]
    for copy in chunks + small:
        copy.start()
    for copy in chunks + small:
        copy.wait()
    low = lax.broadcasted_iota(jnp.int32, (16, 128), 1) < 64
    first4 = jnp.concatenate([first_ref[...]] * 4, axis=0)
    for k in range(4):
        x = x_ref[k * 128 : k * 128 + 128].astype(F32)
        mean = jnp.mean(x, axis=-1, keepdims=True)
        centred = x - mean
        variance = jnp.mean(centred * centred, axis=-1, keepdims=True)
        normed = (centred * lax.rsqrt(variance + 1e-05) * gain_ref[...]).astype(BF16)
        rows_ref[k * 128 : k * 128 + 128] = lax.dot_general(normed, first4, NT, preferred_element_type=F32)
        right = lax.dot_general(second_ref[...], normed, NT, preferred_element_type=F32)
        head, tail = right[:16], right[16:]
        even = jnp.where(low, head, pltpu.roll(tail, 64, 1)).astype(BF16)
        odd = jnp.where(low, pltpu.roll(head, 64, 1), tail).astype(BF16)
        for which, block in ((2 * k, even), (2 * k + 1, odd)):
            for z in range(Z):
                message_ref[PLACE[which // X][z][which % X], 16:, :] = block
    group = lax.broadcasted_iota(jnp.int32, (128, 128), 1) // 32
    left = rows_ref[pl.ds(0, 128, stride=4), :]
    for r in range(1, 4):
        left = jnp.where(group == r, rows_ref[pl.ds(r, 128, stride=4), :], left)
    for z in range(Z):
        block = jnp.concatenate([left[z * 8 : z * 8 + 8], left[64 + z * 8 : 72 + z * 8]], axis=0).astype(BF16)
        for y in range(Y):
            for xx in range(X):
                message_ref[PLACE[y][z][xx], :16, :] = block


def spread_left(core, flat_ref, write):
    for owner in range(8):
        block = flat_ref[pl.ds(owner * 2 + core, 64, stride=32), :]
        both = jnp.concatenate([block, pltpu.roll(block, 96, 1)], axis=0).T.astype(BF16)
        write(owner * 64, both[:32])
        write(owner * 64 + 32, both[64:96])


def spread_right(block):
    low = lax.broadcasted_iota(jnp.int32, (64, 128), 1) < 64
    zero = jnp.zeros((64, 128), F32)
    block = block.astype(F32)
    rolled = pltpu.roll(block, 64, 1)
    upper = jnp.concatenate([jnp.where(low, block, zero), jnp.where(low, rolled, zero)], axis=1)
    lower = jnp.concatenate([jnp.where(low, zero, rolled), jnp.where(low, zero, block)], axis=1)
    return jnp.concatenate([upper, lower], axis=0).astype(BF16)


def share_kernel(core_ref, own_ref, mix_ref, lhs_ref, share_ref, mixer_ref, flat_ref, wide_ref):
    flat_ref[...] = own_ref[...].astype(F32).reshape(64 * 32, 128)

    def write_own(at, value):
        lhs_ref[at : at + 32] = value

    def write_other(at, value):
        share_ref[at : at + 32] = value

    spread_left(core_ref[0], flat_ref, write_own)
    spread_left(1 - core_ref[0], flat_ref, write_other)
    for row in range(16):
        share_ref[512 + row * 64 : 576 + row * 64] = flat_ref[pl.ds(16 + row, 64, stride=32), :].astype(BF16)
    wide_ref[...] = mix_ref[...].astype(F32)
    for e in range(0, 32, 4):
        rows = [wide_ref[pl.ds(e + k, 32, stride=32), :] for k in range(4)]
        mixer_ref[:, e * 32 : e * 32 + 128] = jnp.concatenate(rows, axis=0).T.astype(BF16)


def pair_kernel(core_ref, shares_ref, lhs_ref, share_ref, mixer_ref, offset_ref, out_ref, both_ref, outer_ref):
    other = 1 - core_ref[0]
    both_ref[:, :128] = lhs_ref[...]
    both_ref[:, 128:] = shares_ref[other, :512]
    for row in range(16):
        at = slice(512 + row * 64, 576 + row * 64)
        right = jnp.concatenate([spread_right(share_ref[at]), spread_right(shares_ref[other, at])], axis=0)
        product = jnp.dot(both_ref[...], right, preferred_element_type=F32).astype(BF16)
        for half in range(2):
            e = row + 16 * half
            for owner in range(16):
                outer_ref[e * 32 : e * 32 + 32, owner * 128 : owner * 128 + 128] = product[
                    owner * 32 : owner * 32 + 32, half * 128 : half * 128 + 128
                ]
    for pair in range(8):
        result = jnp.dot(
            mixer_ref[...], outer_ref[:, pair * 256 : pair * 256 + 256], preferred_element_type=F32
        )
        for half in range(2):
            block = result[:, half * 128 : half * 128 + 128].T
            out_ref[pair * 2 + half] = (block * (1.0 / 128) + offset_ref[...]).astype(BF16)


def in_hbm(array):
    return pltpu.with_memory_space_constraint(array, pltpu.HBM)


def body(x, gain, first, second, mix, offset):
    hbm = pl.BlockSpec(memory_space=pltpu.HBM)
    vmem = pl.BlockSpec(memory_space=pltpu.VMEM)
    smem = pl.BlockSpec(memory_space=pltpu.SMEM)
    message, bias = pl.pallas_call(
        project_kernel,
        out_shape=(
            jax.ShapeDtypeStruct((64, 32, 128), BF16),
            jax.ShapeDtypeStruct((1, 128), F32),
        ),
        in_specs=[hbm] * 5,
        out_specs=(vmem, vmem),
        scratch_shapes=[
            pltpu.VMEM((512, 256), BF16),
            pltpu.VMEM((1, 256), F32),
            pltpu.VMEM((32, 256), BF16),
            pltpu.VMEM((32, 256), BF16),
            pltpu.VMEM((512, 128), F32),
            pltpu.SemaphoreType.DMA((8,)),
        ],
        compiler_params=pltpu.CompilerParams(vmem_limit_bytes=32 * MIB),
    )(
        in_hbm(x.reshape(512, 256)),
        in_hbm(gain.reshape(1, 256)),
        in_hbm(first.T),
        in_hbm(second.T),
        in_hbm(offset.reshape(1, 128)),
    )
    message, core = lax.optimization_barrier((message, (lax.axis_index("res") % C).reshape(1)))
    own = lax.all_to_all(message, "res", split_axis=0, concat_axis=0, tiled=True, axis_index_groups=CHIP)
    lhs, share, mixer = pl.pallas_call(
        share_kernel,
        out_shape=(
            jax.ShapeDtypeStruct((512, 128), BF16),
            jax.ShapeDtypeStruct((1536, 128), BF16),
            jax.ShapeDtypeStruct((128, 1024), BF16),
        ),
        in_specs=[smem, vmem, vmem],
        out_specs=(vmem, vmem, vmem),
        scratch_shapes=[pltpu.VMEM((64 * 32, 128), F32), pltpu.VMEM((1024, 128), F32)],
        compiler_params=pltpu.CompilerParams(vmem_limit_bytes=32 * MIB),
    )(core, own, mix)
    shares = lax.all_gather(share, "res", axis=0, tiled=False, axis_index_groups=PAIR)
    tile = pl.pallas_call(
        pair_kernel,
        out_shape=jax.ShapeDtypeStruct((16, 128, 128), BF16),
        in_specs=[smem] + [vmem] * 5,
        out_specs=vmem,
        scratch_shapes=[
            pltpu.VMEM((512, 256), BF16),
            pltpu.VMEM((1024, 2048), BF16),
        ],
        compiler_params=pltpu.CompilerParams(vmem_limit_bytes=32 * MIB),
    )(core, shares, lhs, share, mixer, bias)
    tile = tile.reshape(8, 4, 64, 128)
    got = lax.all_to_all(tile, "res", split_axis=0, concat_axis=0, tiled=True, axis_index_groups=COLUMN)
    return got.transpose(1, 0, 2, 3).reshape(4, 512, 128)


def solution(mesh):
    split = P(("crop", "res"), None, None)
    return jax.shard_map(
        body, mesh=mesh, in_specs=(split, P(), P(), P(), P(), P()), out_specs=split, check_vma=False
    )
```

```python
import jax
import jax.numpy as jnp
from jax import lax
from jax.experimental import pallas as pl
from jax.experimental.pallas import tpu as pltpu
from jax.sharding import PartitionSpec as P

Y, Z, X, C = 2, 8, 4, 2
F32, BF16 = jnp.float32, jnp.bfloat16
ORDER = [(y, z, x) for z in reversed(range(Z)) for y in reversed(range(Y)) for x in range(X)]
PLACE = [[[ORDER.index((y, z, x)) for x in range(X)] for z in range(Z)] for y in range(Y)]
CHIP = [[((y * Z + z) * X + x) * C + c for y, z, x in ORDER] for c in range(C)]
COLUMN = [[((y * Z + z) * X + x) * C + c for y in range(Y) for x in range(X)] for z in range(Z) for c in range(C)]
PAIR = [[2 * k, 2 * k + 1] for k in range(Y * Z * X)]
NT = (((1,), (1,)), ((), ()))
MIB = 1024 * 1024


def project_kernel(x_hbm, gain_hbm, first_hbm, second_hbm, offset_hbm, message_ref, offset_ref, x_ref, gain_ref, first_ref, second_ref, rows_ref, sems):
    small = [
        pltpu.make_async_copy(gain_hbm, gain_ref, sems.at[4]),
        pltpu.make_async_copy(first_hbm, first_ref, sems.at[5]),
        pltpu.make_async_copy(second_hbm, second_ref, sems.at[6]),
        pltpu.make_async_copy(offset_hbm, offset_ref, sems.at[7]),
    ]
    chunks = [
        pltpu.make_async_copy(x_hbm.at[pl.ds(k * 128, 128)], x_ref.at[pl.ds(k * 128, 128)], sems.at[k])
        for k in range(4)
    ]
    for copy in chunks + small:
        copy.start()
    for copy in chunks + small:
        copy.wait()
    low = lax.broadcasted_iota(jnp.int32, (16, 128), 1) < 64
    first4 = jnp.concatenate([first_ref[...]] * 4, axis=0)
    for k in range(4):
        x = x_ref[k * 128 : k * 128 + 128].astype(F32)
        mean = jnp.mean(x, axis=-1, keepdims=True)
        centred = x - mean
        variance = jnp.mean(centred * centred, axis=-1, keepdims=True)
        normed = (centred * lax.rsqrt(variance + 1e-05) * gain_ref[...]).astype(BF16)
        rows_ref[k * 128 : k * 128 + 128] = lax.dot_general(normed, first4, NT, preferred_element_type=F32)
        right = lax.dot_general(second_ref[...], normed, NT, preferred_element_type=F32)
        head, tail = right[:16], right[16:]
        even = jnp.where(low, head, pltpu.roll(tail, 64, 1)).astype(BF16)
        odd = jnp.where(low, pltpu.roll(head, 64, 1), tail).astype(BF16)
        for which, block in ((2 * k, even), (2 * k + 1, odd)):
            for z in range(Z):
                message_ref[PLACE[which // X][z][which % X], 16:, :] = block
    group = lax.broadcasted_iota(jnp.int32, (128, 128), 1) // 32
    left = rows_ref[pl.ds(0, 128, stride=4), :]
    for r in range(1, 4):
        left = jnp.where(group == r, rows_ref[pl.ds(r, 128, stride=4), :], left)
    for z in range(Z):
        block = jnp.concatenate([left[z * 8 : z * 8 + 8], left[64 + z * 8 : 72 + z * 8]], axis=0).astype(BF16)
        for y in range(Y):
            for xx in range(X):
                message_ref[PLACE[y][z][xx], :16, :] = block


def spread_left(core, flat_ref, write):
    for owner in range(8):
        block = flat_ref[pl.ds(owner * 2 + core, 64, stride=32), :]
        both = jnp.concatenate([block, pltpu.roll(block, 96, 1)], axis=0).T.astype(BF16)
        write(owner * 64, both[:32])
        write(owner * 64 + 32, both[64:96])


def spread_right(block):
    low = lax.broadcasted_iota(jnp.int32, (64, 128), 1) < 64
    zero = jnp.zeros((64, 128), F32)
    block = block.astype(F32)
    rolled = pltpu.roll(block, 64, 1)
    upper = jnp.concatenate([jnp.where(low, block, zero), jnp.where(low, rolled, zero)], axis=1)
    lower = jnp.concatenate([jnp.where(low, zero, rolled), jnp.where(low, zero, block)], axis=1)
    return jnp.concatenate([upper, lower], axis=0).astype(BF16)


def share_kernel(core_ref, own_ref, mix_ref, lhs_ref, share_ref, mixer_ref, flat_ref, wide_ref):
    flat_ref[...] = own_ref[...].astype(F32).reshape(64 * 32, 128)

    def write_own(at, value):
        lhs_ref[at : at + 32] = value

    def write_other(at, value):
        share_ref[at : at + 32] = value

    spread_left(core_ref[0], flat_ref, write_own)
    spread_left(1 - core_ref[0], flat_ref, write_other)
    for row in range(16):
        share_ref[512 + row * 64 : 576 + row * 64] = flat_ref[pl.ds(16 + row, 64, stride=32), :].astype(BF16)
    wide_ref[...] = mix_ref[...].astype(F32)
    for e in range(0, 32, 4):
        rows = [wide_ref[pl.ds(e + k, 32, stride=32), :] for k in range(4)]
        mixer_ref[:, e * 32 : e * 32 + 128] = jnp.concatenate(rows, axis=0).T.astype(BF16)


def pair_kernel(core_ref, shares_ref, lhs_ref, share_ref, mixer_ref, offset_ref, out_ref, both_ref, outer_ref):
    other = 1 - core_ref[0]
    both_ref[:, :128] = lhs_ref[...]
    both_ref[:, 128:] = shares_ref[other, :512]
    for row in range(16):
        at = slice(512 + row * 64, 576 + row * 64)
        right = jnp.concatenate([spread_right(share_ref[at]), spread_right(shares_ref[other, at])], axis=0)
        product = jnp.dot(both_ref[...], right, preferred_element_type=F32).astype(BF16)
        for half in range(2):
            e = row + 16 * half
            for owner in range(16):
                outer_ref[e * 32 : e * 32 + 32, owner * 128 : owner * 128 + 128] = product[
                    owner * 32 : owner * 32 + 32, half * 128 : half * 128 + 128
                ]
    for pair in range(8):
        result = jnp.dot(
            mixer_ref[...], outer_ref[:, pair * 256 : pair * 256 + 256], preferred_element_type=F32
        )
        for half in range(2):
            block = result[:, half * 128 : half * 128 + 128].T
            out_ref[pair * 2 + half] = (block * (1.0 / 128) + offset_ref[...]).astype(BF16)


def in_hbm(array):
    return pltpu.with_memory_space_constraint(array, pltpu.HBM)


def body(x, gain, first, second, mix, offset):
    hbm = pl.BlockSpec(memory_space=pltpu.HBM)
    vmem = pl.BlockSpec(memory_space=pltpu.VMEM)
    smem = pl.BlockSpec(memory_space=pltpu.SMEM)
    message, bias = pl.pallas_call(
        project_kernel,
        out_shape=(
            jax.ShapeDtypeStruct((64, 32, 128), BF16),
            jax.ShapeDtypeStruct((1, 128), F32),
        ),
        in_specs=[hbm] * 5,
        out_specs=(vmem, vmem),
        scratch_shapes=[
            pltpu.VMEM((512, 256), BF16),
            pltpu.VMEM((1, 256), F32),
            pltpu.VMEM((32, 256), BF16),
            pltpu.VMEM((32, 256), BF16),
            pltpu.VMEM((512, 128), F32),
            pltpu.SemaphoreType.DMA((8,)),
        ],
        compiler_params=pltpu.CompilerParams(vmem_limit_bytes=32 * MIB),
    )(
        in_hbm(x.reshape(512, 256)),
        in_hbm(gain.reshape(1, 256)),
        in_hbm(first.T),
        in_hbm(second.T),
        in_hbm(offset.reshape(1, 128)),
    )
    message, core = lax.optimization_barrier((message, (lax.axis_index("res") % C).reshape(1)))
    own = lax.all_to_all(message, "res", split_axis=0, concat_axis=0, tiled=True, axis_index_groups=CHIP)
    lhs, share, mixer = pl.pallas_call(
        share_kernel,
        out_shape=(
            jax.ShapeDtypeStruct((512, 128), BF16),
            jax.ShapeDtypeStruct((1536, 128), BF16),
            jax.ShapeDtypeStruct((128, 1024), BF16),
        ),
        in_specs=[smem, vmem, vmem],
        out_specs=(vmem, vmem, vmem),
        scratch_shapes=[pltpu.VMEM((64 * 32, 128), F32), pltpu.VMEM((1024, 128), F32)],
        compiler_params=pltpu.CompilerParams(vmem_limit_bytes=32 * MIB),
    )(core, own, mix)
    shares = lax.all_gather(share, "res", axis=0, tiled=False, axis_index_groups=PAIR)
    tile = pl.pallas_call(
        pair_kernel,
        out_shape=jax.ShapeDtypeStruct((16, 128, 128), BF16),
        in_specs=[smem] + [vmem] * 5,
        out_specs=vmem,
        scratch_shapes=[
            pltpu.VMEM((512, 256), BF16),
            pltpu.VMEM((1024, 2048), BF16),
        ],
        compiler_params=pltpu.CompilerParams(vmem_limit_bytes=32 * MIB),
    )(core, shares, lhs, share, mixer, bias)
    tile = tile.reshape(8, 4, 64, 128)
    got = lax.all_to_all(tile, "res", split_axis=0, concat_axis=0, tiled=True, axis_index_groups=COLUMN)
    return got.transpose(1, 0, 2, 3).reshape(4, 512, 128)


def solution(mesh):
    split = P(("crop", "res"), None, None)
    return jax.shard_map(
        body, mesh=mesh, in_specs=(split, P(), P(), P(), P(), P()), out_specs=split, check_vma=False
    )
```
